512 devices in a mesh: leaf: 512 (over y, x, z, core).
Axes of the slice: x: 4, y: 8, z: 8, core: 2. Of those that a mesh axis runs over, the one named last changes fastest.
Arguments:
- features: bfloat16 [262144, 128], P('leaf'), may hold values from -0.75 to 0.75
- noise: float32 [262144], P('leaf'), may hold values from 0.5 to 2
- targets: float32 [262144, 128], P('leaf'), may hold values from -6 to 6
- anchors: bfloat16 [3, 2, 128, 128], replicated, may hold values from -0.75 to 0.75
- order: int32 [262144], P('leaf'), may hold values from 0 to 262143, as said below
Outputs:
- solved: float32 [262144, 128], P('leaf')
- coupling: float32 [3, 131072, 128], P(None, 'leaf')
The draws below stay inside these ranges and needn't reach their ends.
Inputs may be any that keep to these rules, and one draw needn't show every extreme that they name: `order`: each aligned block of 512 entries is a permutation of that block's own indices.
All inputs are finite; a program needn't handle non-finite values.
Results may differ from the reference program's by a relative error of at most 0.0003.
Values sent between devices are 32-bit elements; how exact they have to be, the bound alone decides.
No kernel may reach another device: no remote copies, remote signals or barrier semaphores. Data moves between devices by JAX's collectives and lax.ppermute only.
A program may use at most 64 MiB of HBM per device.

```python
import math
import jax
import jax.numpy as jnp
from jax import lax

PTS_DEV = 512
FEAT = 128
RANK = 128
LEVELS = 3
NRHS = 128
POINTS = 262144
N_LEAF = 512


def draw_order(key, part):
    key = jax.random.fold_in(key, 11)
    blocks = POINTS // PTS_DEV
    keys = jax.random.split(key, blocks)
    local = jax.vmap(lambda single: jax.random.permutation(single, PTS_DEV))(keys)
    offsets = jnp.arange(blocks, dtype=jnp.int32)[:, None] * PTS_DEV
    return (local.astype(jnp.int32) + offsets).reshape(POINTS).astype(jnp.int32)


def block_levels(stream_key, extent, pieces, least, largest):
    loudness, own = 1.0, jax.random.fold_in(stream_key, 6)
    for dim, shards_of in pieces:
        steps = jnp.exp(jax.random.uniform(jax.random.fold_in(own, dim), (shards_of,), jnp.float32, least / len(pieces), largest / len(pieces)))
        loudness = loudness * jnp.repeat(steps, extent[dim] // shards_of).reshape([-1 if axis == dim else 1 for axis in range(len(extent))])
    return loudness


def bell_draw(key, dims, spread, bound, shards=(), kind=jnp.bfloat16):
    array = jax.random.normal(key, dims, jnp.float32) * spread
    if len(shards) > 0:
        array = block_levels(key, dims, shards, -0.22, 0.18) * array
    return jnp.clip(array, min=-bound, max=bound).astype(kind)


def setup_inputs(seed: int = 0) -> dict:
    arg_keys = jax.random.split(jax.random.key(seed), 6)
    features = bell_draw(arg_keys[0], (POINTS, FEAT), 0.125, 0.75, ((0, 512),))
    noise = jnp.clip(jnp.exp(math.log(2.0) - 1.3862944 * jax.random.uniform(arg_keys[1], (POINTS,), jnp.float32) ** block_levels(arg_keys[1], (POINTS,), ((0, 512),), -0.2, 0.2)), 0.5, 2.0)
    targets = bell_draw(arg_keys[2], (POINTS, NRHS), 1.0, 6.0, ((0, 512),), jnp.float32)
    anchors = bell_draw(arg_keys[3], (LEVELS, 2, RANK, FEAT), 0.125, 0.75)
    order = draw_order(jax.random.fold_in(arg_keys[5], 71), 0)
    return {"features": features, "noise": noise, "targets": targets, "anchors": anchors, "order": order}


length_scale = 0.5
kernel_gain = 64.0

def kernel_panel(points, anchor_set, weight):
    cross = jnp.dot(points.astype(jnp.float32), anchor_set.T.astype(jnp.float32), preferred_element_type=jnp.float32)
    point_norm = lax.optimization_barrier(jnp.sum(points.astype(jnp.float32) ** 2, axis=1, keepdims=True))
    anchor_norm = lax.optimization_barrier(jnp.sum(anchor_set.astype(jnp.float32) ** 2, axis=1))[None, :]
    distance = jnp.sqrt(point_norm + anchor_norm - 2.0 * cross)
    scaled = math.sqrt(3.0) * distance / length_scale
    return weight * (1.0 + scaled) * jnp.exp(-scaled)

def reference(features, noise, targets, anchors, order):
    top = N_LEAF.bit_length() - 1
    width = 2 * RANK
    points = features[order]
    inverse = 1.0 / noise[order]
    rhs = targets[order]
    device = jnp.arange(POINTS, dtype=jnp.int32) // PTS_DEV
    panels = []
    for level in range(LEVELS):
        bit = top - LEVELS + level
        side = device >> bit & 1
        weight = kernel_gain / math.sqrt(PTS_DEV * 2 ** (bit + 1))
        both = jnp.concatenate([anchors[level, 0], anchors[level, 1]], axis=0)
        values = kernel_panel(points, both, weight)
        swapped = jnp.concatenate([values[:, RANK:], values[:, :RANK]], axis=1)
        panels.append(jnp.where(side[:, None] == 0, values, swapped))
    states = [panel * inverse[:, None] for panel in panels]
    solved = rhs * inverse[:, None]
    coefs = []
    for level in range(LEVELS):
        bit = top - LEVELS + level
        groups = N_LEAF >> bit + 1
        count = POINTS // groups
        stack = jnp.concatenate(states[level:] + [solved], axis=1)
        grouped_panel = panels[level].reshape(groups, count, width)
        grouped_stack = stack.reshape(groups, count, stack.shape[1])
        total = jnp.einsum('gnr,gnc->grc', grouped_panel, grouped_stack, precision=lax.Precision.HIGHEST)
        core = jnp.eye(width, dtype=jnp.float32)[None] + total[:, :, :width]
        factor = jnp.linalg.cholesky(core)
        mixed = jax.vmap(lambda fac, rest: jax.scipy.linalg.cho_solve((fac, True), rest))(factor, total[:, :, width:])
        update = jnp.einsum('gnr,grc->gnc', states[level].reshape(groups, count, width), mixed, precision=lax.Precision.HIGHEST).reshape(POINTS, mixed.shape[2])
        for later in range(level + 1, LEVELS):
            start = (later - level - 1) * width
            states[later] = states[later] - update[:, start:start + width]
        solved = solved - update[:, -NRHS:]
        copies = jnp.repeat(mixed[:, :, -NRHS:], N_LEAF // groups, axis=0)
        coefs.append(copies.reshape(N_LEAF * width, NRHS))
    return (solved, jnp.stack(coefs))
```

```python
import math

import jax
import jax.numpy as jnp
import numpy as np
from jax import lax
from jax.experimental import pallas as pl
from jax.experimental.pallas import tpu as pltpu
from jax.sharding import PartitionSpec as P

PTS = 512
BLK = 128
WIDTH = 256
LEVELS = 3
KERNEL_GAIN = 64.0
TOP = 9
PAIRS = [
    [(i, j) for i, j in ((a, b) for a in (2 * l, 2 * l + 1) for b in range(a, 7))]
    for l in range(LEVELS)
]
COUNTS = [len(p) for p in PAIRS]
ROWS = [8 * c for c in COUNTS]
TOTAL = sum(ROWS)
NEWTON_LIMIT = 3.0e4
HIGHEST = lax.Precision.HIGHEST
VMEM = pl.BlockSpec(memory_space=pltpu.VMEM)
PARAMS = pltpu.CompilerParams(vmem_limit_bytes=48 * 2**20)


def dot(a, b, dims=((1,), (0,)), precision=HIGHEST):
    return lax.dot_general(a, b, (dims, ((), ())), precision=precision, preferred_element_type=jnp.float32)


def gram_kernel(noise_ref, feat_ref, targ_ref, anch_ref, gram_ref, panel_ref, scaled_ref):
    device = lax.axis_index("leaf")
    core = device & 1
    inverse = 1.0 / noise_ref[...]
    feats = feat_ref[...]
    wide = feats.astype(jnp.float32)
    point_norm = dot(jnp.ones((8, BLK), jnp.float32), wide * wide, ((1,), (1,)))[:1]
    for level in range(LEVELS):
        bit = TOP - LEVELS + level
        side = (device >> bit) & 1
        weight = KERNEL_GAIN / math.sqrt(PTS * 2 ** (bit + 1))
        for which in range(2):
            anchors = anch_ref[level, side ^ which]
            cross = dot(anchors, feats, ((1,), (1,)), None)
            a32 = anchors.astype(jnp.float32)
            anchor_norm = jnp.sum(a32 * a32, axis=1, keepdims=True)
            squared = point_norm + anchor_norm - 2.0 * cross
            scaled = jnp.sqrt(12.0 * jnp.maximum(squared, 0.0))
            values = weight * (1.0 + scaled) * jnp.exp(-scaled)
            at = BLK * (2 * level + which)
            panel_ref[at : at + BLK, :] = values
            scaled_ref[at : at + BLK, :] = values * inverse
    targets = targ_ref[...]
    place = 0
    for i in range(2 * LEVELS):
        left = panel_ref[BLK * i : BLK * (i + 1), :]
        right = scaled_ref[BLK * i :, :]
        products = dot(left, right, ((1,), (1,)))
        rhs = dot(scaled_ref[BLK * i : BLK * (i + 1), :], targets)
        for j in range(i, 7):
            block = rhs if j == 6 else products[:, BLK * (j - i) : BLK * (j - i + 1)]
            block = block.reshape(2, 8, 8, BLK)
            gram_ref[core, :, place : place + 8, :] = block[0]
            gram_ref[1 - core, :, place : place + 8, :] = block[1]
            place += 8


def gram(noise, features, targets, anchors):
    return pl.pallas_call(
        gram_kernel,
        out_shape=(
            jax.ShapeDtypeStruct((2, 8, TOTAL, BLK), jnp.float32),
            jax.ShapeDtypeStruct((2 * LEVELS * BLK, PTS), jnp.float32),
        ),
        in_specs=[VMEM] * 4,
        out_specs=(VMEM, VMEM),
        scratch_shapes=[pltpu.VMEM((2 * LEVELS * BLK, PTS), jnp.float32)],
        compiler_params=PARAMS,
    )(noise.reshape(1, PTS), features, targets, anchors)


def load_blocks(level, own_ref, other_ref, core, a_ref, b_ref):
    half = 64
    for k, (i, j) in enumerate(PAIRS[level]):
        row = BLK * (i - 2 * level)
        column = BLK * (j - 2 * level)
        dst, column = (a_ref, column) if column < WIDTH else (b_ref, column - WIDTH)
        for ref, which in ((own_ref, core), (other_ref, 1 - core)):
            at = pl.multiple_of(row + half * which, half)
            dst[pl.ds(at, half), column : column + BLK] = ref[:, 8 * k : 8 * k + 8, :].reshape(half, BLK)
    a_ref[BLK:, :BLK] = a_ref[:BLK, BLK:].T
    a_ref[...] = a_ref[...] + identity()


def identity():
    rows = lax.broadcasted_iota(jnp.int32, (WIDTH, WIDTH), 0)
    columns = lax.broadcasted_iota(jnp.int32, (WIDTH, WIDTH), 1)
    return jnp.where(rows == columns, 1.0, 0.0).astype(jnp.float32)


def invert(a_ref, x_ref):
    a = a_ref[...]
    bound = jnp.max(jnp.sum(jnp.abs(a), axis=0, keepdims=True))

    @pl.when(bound <= NEWTON_LIMIT)
    def _newton():
        low = 2.0 / (1.0 + bound)
        after = low * (2.0 - low)
        scale = 2.0 / (1.0 + after)
        x_ref[...] = (scale * low) * (2.0 * identity() - low * a)

        def more(state):
            return state[0] < 1.0 - 3e-7

        def step(state):
            low = state[0]
            after = low * (2.0 - low)
            scale = 2.0 / (1.0 + after)
            x = x_ref[...]
            rest = 2.0 * identity() - dot(a_ref[...], x)
            x_ref[...] = scale * dot(x, rest)
            return (scale * after,)

        lax.while_loop(more, step, (scale * after,))

    @pl.when(jnp.logical_not(bound <= NEWTON_LIMIT))
    def _direct():
        x_ref[...] = a
        lanes = lax.broadcasted_iota(jnp.int32, (1, WIDTH), 1)
        rows = lax.broadcasted_iota(jnp.int32, (WIDTH, 1), 0)

        def step(k, carry):
            x = x_ref[...]
            row = jnp.sum(jnp.where(rows == k, x, 0.0), axis=0, keepdims=True)
            column = jnp.sum(jnp.where(lanes == k, x, 0.0), axis=1, keepdims=True)
            pivot = jnp.sum(jnp.where(lanes == k, row, 0.0), axis=1, keepdims=True)
            row = jnp.where(lanes == k, 1.0, row) / pivot
            cleared = jnp.where(lanes == k, 0.0, x)
            x_ref[...] = jnp.where(rows == k, row, cleared - column * row)
            return carry

        lax.fori_loop(0, WIDTH, step, 0)


def level_kernel(level, own_ref, other_ref, rest_ref, coef_ref, new_ref, a_ref, x_ref, b_ref, t_ref):
    device = lax.axis_index("leaf")
    core = device & 1
    piece = 8 * core + 4 * ((device >> 6) & 1) + ((device >> 4) & 3)
    load_blocks(level, own_ref, other_ref, core, a_ref, b_ref)
    invert(a_ref, x_ref)
    coef_ref[...] = dot(x_ref[...], b_ref[...])
    blocks = 2 * (LEVELS - 1 - level)
    for k in range(blocks):
        t_ref[k * BLK : (k + 1) * BLK, :] = b_ref[:, k * BLK : (k + 1) * BLK].T
    mine = jnp.concatenate(
        [t_ref[pl.ds(pl.multiple_of(k * BLK + 8 * piece, 8), 8), :] for k in range(blocks)], axis=0
    )
    change = dot(mine, coef_ref[...])
    place = 0
    for later in range(level + 1, LEVELS):
        for i, j in PAIRS[later]:
            row = 8 * (i - 2 * (level + 1))
            column = BLK * (j - 2 * (level + 1))
            new_ref[place : place + 8, :] = (
                rest_ref[place : place + 8, :] - change[row : row + 8, column : column + BLK]
            )
            place += 8


def solve_level(level, own, other, rest):
    columns = WIDTH * (LEVELS - 1 - level) + BLK
    return pl.pallas_call(
        lambda *refs: level_kernel(level, *refs),
        out_shape=(
            jax.ShapeDtypeStruct((WIDTH, columns), jnp.float32),
            jax.ShapeDtypeStruct(rest.shape, jnp.float32),
        ),
        in_specs=[VMEM] * 3,
        out_specs=(VMEM, VMEM),
        scratch_shapes=[
            pltpu.VMEM((WIDTH, WIDTH), jnp.float32),
            pltpu.VMEM((WIDTH, WIDTH), jnp.float32),
            pltpu.VMEM((WIDTH, columns), jnp.float32),
            pltpu.VMEM((columns - BLK, WIDTH), jnp.float32),
        ],
        compiler_params=PARAMS,
    )(own, other, rest)


def split3(value):
    first = value.astype(jnp.bfloat16)
    left = value - first.astype(jnp.float32)
    second = left.astype(jnp.bfloat16)
    third = (left - second.astype(jnp.float32)).astype(jnp.bfloat16)
    return first, second, third


def as_column(row, k):
    return jnp.broadcast_to(row[:, BLK * k : BLK * (k + 1)], (BLK, BLK)).T


def last_kernel(
    own_ref, other_ref, coef0_ref, coef1_ref, panel_ref, noise_ref, targ_ref, order_ref,
    solved_ref, coupling_ref, a_ref, x_ref, b_ref, z_ref,
):
    device = lax.axis_index("leaf")
    core = device & 1
    load_blocks(LEVELS - 1, own_ref, other_ref, core, a_ref, b_ref)
    invert(a_ref, x_ref)
    z2 = dot(x_ref[...], b_ref[...])
    z1 = coef1_ref[:, WIDTH:] - dot(coef1_ref[:, :WIDTH], z2)
    z_ref[WIDTH : 2 * WIDTH, :] = z1
    z_ref[2 * WIDTH :, :] = z2
    z0 = coef0_ref[:, 2 * WIDTH :] - dot(coef0_ref[:, : 2 * WIDTH], z_ref[WIDTH:, :])
    z_ref[:WIDTH, :] = z0
    coupling_ref[0] = coef0_ref[:, 2 * WIDTH :]
    coupling_ref[1] = coef1_ref[:, WIDTH:]
    coupling_ref[2] = z2
    left = targ_ref[...] - dot(panel_ref[...], z_ref[...], ((0,), (0,)))
    inverse = 1.0 / noise_ref[...]
    local = order_ref[...] - device * PTS
    left = left * jnp.concatenate([as_column(inverse, k) for k in range(4)], axis=0)
    pieces = jnp.concatenate(split3(left), axis=1)
    lanes = lax.broadcasted_iota(jnp.int32, (BLK, PTS), 1).astype(jnp.float32)
    for k in range(4):
        wanted = as_column(local.astype(jnp.float32), k)
        wanted = jnp.concatenate([wanted] * 4, axis=1)
        pick = jnp.where(wanted == lanes, 1.0, 0.0).astype(jnp.bfloat16)
        moved = dot(pick, pieces, precision=None)
        solved_ref[BLK * k : BLK * (k + 1), :] = (moved[:, :BLK] + moved[:, BLK : 2 * BLK]) + moved[:, 2 * BLK :]


def solve_last(own, other, coef0, coef1, panel, noise, targets, order):
    return pl.pallas_call(
        last_kernel,
        out_shape=(
            jax.ShapeDtypeStruct((PTS, BLK), jnp.float32),
            jax.ShapeDtypeStruct((LEVELS, WIDTH, BLK), jnp.float32),
        ),
        in_specs=[VMEM] * 8,
        out_specs=(VMEM, VMEM),
        scratch_shapes=[
            pltpu.VMEM((WIDTH, WIDTH), jnp.float32),
            pltpu.VMEM((WIDTH, WIDTH), jnp.float32),
            pltpu.VMEM((WIDTH, BLK), jnp.float32),
            pltpu.VMEM((LEVELS * WIDTH, BLK), jnp.float32),
        ],
        compiler_params=PARAMS,
    )(own, other, coef0, coef1, panel, noise.reshape(1, PTS), targets, order.reshape(1, PTS))


GRID = np.arange(512).reshape(4, 2, 4, 8, 2)
PLANE = GRID.transpose(0, 3, 4, 1, 2).reshape(-1, 8).tolist()


def partner(value, bit):
    return lax.ppermute(value, "leaf", [(i, i ^ (1 << bit)) for i in range(512)])


def exchange(value):
    return lax.all_to_all(value, "leaf", 0, 0, axis_index_groups=PLANE)


def gather_rows(rows):
    own = exchange(jnp.broadcast_to(rows[None], (8, *rows.shape)))
    return own, partner(own, 0)


def on_device(features, noise, targets, anchors, order):
    both, panel = gram(noise, features, targets, anchors)
    half = both[0] + partner(both[1], 0)
    rows = jnp.sum(exchange(half), axis=0)
    for bit in (1, 2, 3):
        rows = rows + partner(rows, bit)
    own, other = gather_rows(rows[: ROWS[0]])
    coef0, rest = solve_level(0, own, other, rows[ROWS[0] :])
    rest = rest + partner(rest, 7)
    own, other = gather_rows(rest[: ROWS[1]])
    coef1, rest = solve_level(1, own, other, rest[ROWS[1] :])
    rest = rest + partner(rest, 8)
    own, other = gather_rows(rest)
    return solve_last(own, other, coef0, coef1, panel, noise, targets, order)


def solution(mesh):
    in_specs = (P("leaf", None), P("leaf"), P("leaf", None), P(), P("leaf"))
    out_specs = (P("leaf", None), P(None, "leaf", None))
    return jax.shard_map(on_device, mesh=mesh, in_specs=in_specs, out_specs=out_specs, check_vma=False)
```
